32 devices in a mesh: tm: 8 (over y, x, core), ctr: 4 (over z).
Axes of the slice: x: 2, y: 2, z: 4, core: 2. Of those that a mesh axis runs over, the one named last changes fastest.
Arguments:
- target: float32 [64, 262144], P('ctr', 'tm'), may hold values from -6 to 6
- sparse: float32 [64, 262144], P('ctr', 'tm'), may hold values from -6 to 6
- kernel: float32 [64, 262144], P('ctr', 'tm'), may hold values from -0.03314563 to 0.03314563
- penalty: float32 [64], P('ctr'), may hold values from 0.5 to 5
Outputs:
- updated: float32 [64, 262144], P('ctr', 'tm')
- residual: float32 [64, 262144], P('ctr', 'tm')
- objective: float32 [], replicated
The draws below stay inside these ranges and needn't reach their ends.
All inputs are finite; a program needn't handle non-finite values.
Results may differ from the reference program's by a relative error of at most 0.0003.
Values sent between devices are 32-bit elements; how exact they have to be, the bound alone decides.
A program may use at most 128 MiB of HBM per device.

```python
import math
import jax
import jax.numpy as jnp
from jax import lax

LENGTH = 262144
CTR_DEV = 16
COUNTERS = 64


def draw_kernel(key, part):
    rate_key = jax.random.fold_in(key, 11)
    value_key = jax.random.fold_in(key, 23)
    rates = jnp.exp(jax.random.uniform(rate_key, (COUNTERS, 1), jnp.float32, math.log(0.5), math.log(4.0)))
    position = jnp.arange(LENGTH, dtype=jnp.float32)[None, :] / LENGTH
    norming = jnp.sqrt(2.0 * rates / (LENGTH * (1.0 - jnp.exp(-2.0 * rates))))
    envelope = jnp.exp(-rates * position) * norming
    values = jax.random.truncated_normal(value_key, -6.0, 6.0, (COUNTERS, LENGTH), jnp.float32)
    return (values * envelope).astype(jnp.float32)


def levels(key, shape, split, smallest, top_value):
    def one(axis_at, shards_of):
        steps = jax.random.uniform(jax.random.fold_in(jax.random.fold_in(key, 6), axis_at), (shards_of,), jnp.float32, smallest / len(split), top_value / len(split))
        return jnp.repeat(jnp.exp(steps), shape[axis_at] // shards_of).reshape((-1,) + (1,) * (len(shape) - axis_at - 1))

    loudness = one(*split[0])
    for cut in split[1:]:
        loudness = loudness * one(*cut)
    return loudness


def bell_draw(stream_key, shape, scale, reach, cuts=(), held_as=jnp.bfloat16):
    drawn = jax.random.normal(stream_key, shape, jnp.float32) * scale
    if len(cuts) > 0:
        drawn = levels(stream_key, shape, cuts, -0.22, 0.18) * drawn
    return jnp.clip(drawn, min=-reach, max=reach).astype(held_as)


def setup_inputs(seed: int = 0) -> dict:
    streams_of = jax.random.split(jax.random.key(seed), 5)
    target = bell_draw(streams_of[0], (COUNTERS, LENGTH), 1.0, 6.0, ((0, 4), (1, 8)), jnp.float32)
    sparse = bell_draw(streams_of[1], (COUNTERS, LENGTH), 1.0, 6.0, ((0, 4), (1, 8)), jnp.float32)
    kernel = draw_kernel(jax.random.fold_in(streams_of[4], 71), 0)
    penalty = jnp.clip(jnp.exp(math.log(5.0) - 2.3025851 * jax.random.uniform(streams_of[3], (COUNTERS,), jnp.float32) ** levels(streams_of[3], (COUNTERS,), ((0, 4),), -0.2, 0.2)), 0.5, 5.0)
    return {"target": target, "sparse": sparse, "kernel": kernel, "penalty": penalty}


def reference(target, sparse, kernel, penalty):
    blocks = COUNTERS // CTR_DEV

    def one_block(pieces):
        target_block, sparse_block, kernel_block, penalty_block = pieces
        kernel_freq = jnp.fft.rfft(kernel_block, axis=1)
        sparse_freq = jnp.fft.rfft(sparse_block, axis=1)
        target_freq = jnp.fft.rfft(target_block, axis=1)
        resid_freq = target_freq - kernel_freq * sparse_freq
        grad_freq = jnp.conj(kernel_freq) * resid_freq
        residual = jnp.fft.irfft(resid_freq, n=LENGTH, axis=1).astype(jnp.float32)
        gradient = jnp.fft.irfft(grad_freq, n=LENGTH, axis=1).astype(jnp.float32)
        power = (jnp.real(kernel_freq) ** 2 + jnp.imag(kernel_freq) ** 2).astype(jnp.float32)
        step_size = 1.0 / jnp.max(power, axis=1)
        shifted = sparse_block + step_size[:, None] * gradient
        updated = jnp.sign(shifted) * jnp.maximum(jnp.abs(shifted) - (step_size * penalty_block)[:, None], 0.0)
        partial_value = 0.5 * jnp.sum(residual * residual) + jnp.sum(penalty_block[:, None] * jnp.abs(sparse_block))
        return updated.astype(jnp.float32), residual, partial_value.astype(jnp.float32)

    results = lax.map(one_block, (target.reshape(blocks, CTR_DEV, LENGTH), sparse.reshape(blocks, CTR_DEV, LENGTH),
                                  kernel.reshape(blocks, CTR_DEV, LENGTH), penalty.reshape(blocks, CTR_DEV)))
    updated = results[0].reshape(COUNTERS, LENGTH)
    residual = results[1].reshape(COUNTERS, LENGTH)
    objective = jnp.sum(results[2]) / (COUNTERS * LENGTH)
    return updated, residual, objective
```

```python
import functools

import jax
import jax.numpy as jnp
import ml_dtypes
import numpy as np
from jax import lax
from jax.experimental import pallas as pl
from jax.experimental.pallas import tpu as pltpu
from jax.sharding import PartitionSpec as P

FACTOR = 512
HALF = FACTOR // 2
ROWS = HALF + 16
TILE = 256

KERNEL, SPARSE, TARGET = 0, 1, 2


def split_table(table):
    high = table.astype(ml_dtypes.bfloat16)
    low = (table - high.astype(np.float64)).astype(ml_dtypes.bfloat16)
    return np.stack((high, low))


def make_tables():
    length = FACTOR * FACTOR
    ramp = np.arange(FACTOR)
    angle = (ramp[:, None] * ramp[None, :] % FACTOR) * (2.0 * np.pi / FACTOR)
    cos_table, sin_table = np.cos(angle), np.sin(angle)
    first = np.concatenate((cos_table[:ROWS], -sin_table[:ROWS]), 0)
    second = np.concatenate(
        (
            np.concatenate((cos_table, sin_table), 1),
            np.concatenate((sin_table, -cos_table), 1),
        ),
        0,
    )
    cos_half = 2.0 * cos_table[:, :HALF]
    cos_half[:, 0] = 1.0
    sin_half = -2.0 * sin_table[:, :HALF]
    sin_half[:, 0] = cos_table[:, HALF]
    last = np.concatenate((cos_half, sin_half), 1) / length
    twist = (np.arange(ROWS)[:, None] * ramp[None, :]) * (2.0 * np.pi / length)
    turn = np.stack((np.cos(twist), np.sin(twist))).astype(np.float32)
    return split_table(first), split_table(second), split_table(last), turn


def halves(value):
    high = value.astype(jnp.bfloat16)
    low = (value - high.astype(jnp.float32)).astype(jnp.bfloat16)
    return high, low


def dot3(left, right):
    (left_high, left_low), (right_high, right_low) = left, right
    dot = functools.partial(jnp.dot, preferred_element_type=jnp.float32)
    return dot(left_high, right_high) + (dot(left_low, right_high) + dot(left_high, right_low))


def body(
    parts,
    each,
    block_rows,
    kernel_in,
    sparse_in,
    target_in,
    penalty_in,
    first_in,
    second_in,
    last_in,
    turn_in,
    updated_out,
    residual_out,
    terms_out,
    held,
    spectra,
    mid_high,
    mid_low,
    back_high,
    back_low,
    done,
    first,
    second,
    last,
    turn,
    table_sem,
    in_send,
    in_recv,
    out_send,
    out_recv,
):
    me = lax.axis_index("tm")
    my_rows = pl.ds(pl.multiple_of(me * block_rows, block_rows), block_rows)
    inputs = (kernel_in, sparse_in, target_in)
    outputs = (residual_out, updated_out)

    def peer_rows(peer):
        return pl.ds(pl.multiple_of(peer * block_rows, block_rows), block_rows)

    def send_in(series, j, step):
        peer = lax.rem(me + step, parts)
        return pltpu.make_async_remote_copy(
            src_ref=inputs[series].at[peer * each + j],
            dst_ref=held.at[series, j, my_rows],
            send_sem=in_send.at[series, j, step],
            recv_sem=in_recv.at[series, j, step],
            device_id={"tm": peer},
            device_id_type=pl.DeviceIdType.MESH,
        )

    def own_in(series, j):
        return pltpu.make_async_copy(
            inputs[series].at[me * each + j], held.at[series, j, my_rows], in_recv.at[series, j, 0]
        )

    def send_out(which, j, step):
        peer = lax.rem(me + step, parts)
        return pltpu.make_async_remote_copy(
            src_ref=done.at[which, j, peer_rows(peer)],
            dst_ref=outputs[which].at[me * each + j],
            send_sem=out_send.at[which, j, step],
            recv_sem=out_recv.at[which, j, step],
            device_id={"tm": peer},
            device_id_type=pl.DeviceIdType.MESH,
        )

    def own_out(which, j):
        return pltpu.make_async_copy(
            done.at[which, j, my_rows], outputs[which].at[me * each + j], out_recv.at[which, j, 0]
        )

    tables = (
        pltpu.make_async_copy(first_in, first, table_sem.at[0]),
        pltpu.make_async_copy(second_in, second, table_sem.at[1]),
        pltpu.make_async_copy(last_in, last, table_sem.at[2]),
        pltpu.make_async_copy(turn_in, turn, table_sem.at[3]),
    )
    barrier = pltpu.get_barrier_semaphore()

    @pl.loop(1, parts)
    def _(step):
        pl.semaphore_signal(
            barrier,
            inc=1,
            device_id={"tm": lax.rem(me + step, parts)},
            device_id_type=pl.DeviceIdType.MESH,
        )

    pl.semaphore_wait(barrier, parts - 1)

    @pl.loop(0, each)
    def _(j):
        for series in range(3):

            @pl.loop(1, parts)
            def _(step):
                send_in(series, j, step).start()

            own_in(series, j).start()

    for table in tables:
        table.start()
    terms_out[...] = jnp.zeros_like(terms_out)
    for table in tables:
        table.wait()

    def forward(series, j):
        own_in(series, j).wait()

        @pl.loop(1, parts)
        def _(step):
            send_in(series, j, step).wait_recv()

        for at in range(FACTOR // TILE):
            here = pl.ds(at * TILE, TILE)
            there = pl.ds(FACTOR + at * TILE, TILE)
            part = dot3((first[0], first[1]), halves(held[series, j, :, here]))
            real_part, imag_part = part[:ROWS], part[ROWS:]
            turn_cos, turn_sin = turn[0, :, here], turn[1, :, here]
            mid_high[:, here], mid_low[:, here] = halves(real_part * turn_cos + imag_part * turn_sin)
            mid_high[:, there], mid_low[:, there] = halves(
                imag_part * turn_cos - real_part * turn_sin
            )

        @pl.loop(0, 2 * FACTOR // TILE)
        def _(at):
            here = pl.ds(pl.multiple_of(at * TILE, TILE), TILE)
            spectra[series, :, here] = dot3(
                (mid_high[...], mid_low[...]), (second[0, :, here], second[1, :, here])
            )

    def spectral(at, peak):
        rows = pl.ds(pl.multiple_of(at * 16, 16), 16)
        even, odd = pl.ds(0, FACTOR), pl.ds(FACTOR, FACTOR)
        kernel_even, kernel_odd = spectra[KERNEL, rows, even], spectra[KERNEL, rows, odd]
        sparse_even, sparse_odd = spectra[SPARSE, rows, even], spectra[SPARSE, rows, odd]
        target_even, target_odd = spectra[TARGET, rows, even], spectra[TARGET, rows, odd]
        resid_even = target_even - (kernel_even * sparse_even - kernel_odd * sparse_odd)
        resid_odd = target_odd - (kernel_even * sparse_odd + kernel_odd * sparse_even)
        grad_even = kernel_even * resid_even + kernel_odd * resid_odd
        grad_odd = kernel_even * resid_odd - kernel_odd * resid_even
        back_high[0, rows, even], back_low[0, rows, even] = halves(resid_even)
        back_high[0, rows, odd], back_low[0, rows, odd] = halves(resid_odd)
        back_high[1, rows, even], back_low[1, rows, even] = halves(grad_even)
        back_high[1, rows, odd], back_low[1, rows, odd] = halves(grad_odd)
        return jnp.maximum(peak, kernel_even * kernel_even + kernel_odd * kernel_odd)

    def inverse(which, at):
        here = pl.ds(pl.multiple_of(at * TILE, TILE), TILE)
        there = pl.ds(pl.multiple_of(FACTOR + at * TILE, TILE), TILE)
        both = (back_high[which], back_low[which])
        real_part = dot3(both, (second[0, :, here], second[1, :, here]))
        imag_part = dot3(both, (second[0, :, there], second[1, :, there]))
        turn_cos, turn_sin = turn[0, :, here], turn[1, :, here]
        turned_real = real_part * turn_cos - imag_part * turn_sin
        turned_imag = (real_part * turn_sin + imag_part * turn_cos)[:HALF]
        row = lax.broadcasted_iota(jnp.int32, (HALF, TILE), 0)
        turned_imag = jnp.where(row == 0, turned_real[HALF : HALF + 1], turned_imag)
        packed = jnp.concatenate((turned_real[:HALF], turned_imag), 0)
        return here, dot3((last[0], last[1]), halves(packed))

    @pl.loop(0, each)
    def _(j):
        for series in range(3):
            forward(series, j)
        peak = lax.fori_loop(0, ROWS // 16, spectral, jnp.zeros((16, FACTOR), jnp.float32))
        peak = jnp.max(jnp.max(peak, axis=0, keepdims=True), axis=1, keepdims=True)
        step_size = 1.0 / peak
        penalty = penalty_in[j][0:1, 0:1]
        limit = step_size * penalty

        @pl.loop(0, FACTOR // TILE)
        def _(at):
            here, residual = inverse(0, at)
            done[0, j, :, here] = residual
            terms_out[0:1, here] += jnp.sum(
                0.5 * (residual * residual) + penalty * jnp.abs(held[SPARSE, j, :, here]),
                axis=0,
                keepdims=True,
            )

        @pl.loop(1, parts)
        def _(step):
            send_out(0, j, step).start()

        own_out(0, j).start()

        @pl.loop(0, FACTOR // TILE)
        def _(at):
            here, gradient = inverse(1, at)
            moved = held[SPARSE, j, :, here] + step_size * gradient
            done[1, j, :, here] = moved - jnp.minimum(jnp.maximum(moved, -limit), limit)

        @pl.loop(1, parts)
        def _(step):
            send_out(1, j, step).start()

        own_out(1, j).start()

    @pl.loop(0, each)
    def _(j):
        for series in range(3):

            @pl.loop(1, parts)
            def _(step):
                send_in(series, j, step).wait_send()

        for which in range(2):
            own_out(which, j).wait()

            @pl.loop(1, parts)
            def _(step):
                send_out(which, j, step).wait()


def shards(target, sparse, kernel, penalty):
    parts = lax.axis_size("tm")
    me = lax.axis_index("tm")
    counters, span = sparse.shape
    each = counters // parts
    block_rows = span // FACTOR
    first, second, last, turn = make_tables()
    tiled = [x.reshape(counters, block_rows, FACTOR) for x in (kernel, sparse, target)]
    mine = lax.dynamic_slice(penalty, (me * each,), (each,))
    mine = jnp.broadcast_to(mine[:, None, None], (each, 8, 128))
    anywhere = pl.BlockSpec(memory_space=pl.ANY)
    in_vmem = pl.BlockSpec(memory_space=pltpu.VMEM)
    block = jax.ShapeDtypeStruct((counters, block_rows, FACTOR), jnp.float32)
    bf16, f32 = jnp.bfloat16, jnp.float32
    updated, residual, terms = pl.pallas_call(
        functools.partial(body, parts, each, block_rows),
        out_shape=(block, block, jax.ShapeDtypeStruct((8, FACTOR), f32)),
        in_specs=[anywhere] * 3 + [in_vmem] + [anywhere] * 4,
        out_specs=(anywhere, anywhere, in_vmem),
        scratch_shapes=[
            pltpu.VMEM((3, each, FACTOR, FACTOR), f32),
            pltpu.VMEM((3, ROWS, 2 * FACTOR), f32),
            pltpu.VMEM((ROWS, 2 * FACTOR), bf16),
            pltpu.VMEM((ROWS, 2 * FACTOR), bf16),
            pltpu.VMEM((2, ROWS, 2 * FACTOR), bf16),
            pltpu.VMEM((2, ROWS, 2 * FACTOR), bf16),
            pltpu.VMEM((2, each, FACTOR, FACTOR), f32),
            pltpu.VMEM(first.shape, bf16),
            pltpu.VMEM(second.shape, bf16),
            pltpu.VMEM(last.shape, bf16),
            pltpu.VMEM(turn.shape, f32),
            pltpu.SemaphoreType.DMA((4,)),
            pltpu.SemaphoreType.DMA((3, each, parts)),
            pltpu.SemaphoreType.DMA((3, each, parts)),
            pltpu.SemaphoreType.DMA((2, each, parts)),
            pltpu.SemaphoreType.DMA((2, each, parts)),
        ],
        compiler_params=pltpu.CompilerParams(
            collective_id=0, has_side_effects=True, vmem_limit_bytes=48 * 2**20
        ),
        cost_estimate=pl.CostEstimate(
            flops=30 * 10**9, bytes_accessed=30 * 10**6, transcendentals=0
        ),
    )(*tiled, mine, first, second, last, turn)
    total = lax.psum(jnp.sum(terms), ("tm", "ctr"))
    objective = total / (span * parts * counters * lax.axis_size("ctr"))
    return (
        updated.reshape(counters, span),
        residual.reshape(counters, span),
        objective,
    )


def solution(mesh):
    placed = (P("ctr", "tm"), P("ctr", "tm"), P("ctr", "tm"), P("ctr"))
    return jax.shard_map(
        shards,
        mesh=mesh,
        in_specs=placed,
        out_specs=(P("ctr", "tm"), P("ctr", "tm"), P()),
        check_vma=False,
    )
```

```python
import functools

import jax
import jax.numpy as jnp
import ml_dtypes
import numpy as np
from jax import lax
from jax.experimental import pallas as pl
from jax.experimental.pallas import tpu as pltpu
from jax.sharding import PartitionSpec as P

FACTOR = 512
HALF = FACTOR // 2
ROWS = HALF + 16
TILE = 256

KERNEL, SPARSE, TARGET = 0, 1, 2


def split_table(table):
    high = table.astype(ml_dtypes.bfloat16)
    low = (table - high.astype(np.float64)).astype(ml_dtypes.bfloat16)
    return np.stack((high, low))


def make_tables():
    length = FACTOR * FACTOR
    ramp = np.arange(FACTOR)
    angle = (ramp[:, None] * ramp[None, :] % FACTOR) * (2.0 * np.pi / FACTOR)
    cos_table, sin_table = np.cos(angle), np.sin(angle)
    first = np.concatenate((cos_table[:ROWS], -sin_table[:ROWS]), 0)
    second = np.concatenate(
        (
            np.concatenate((cos_table, sin_table), 1),
            np.concatenate((sin_table, -cos_table), 1),
        ),
        0,
    )
    cos_half = 2.0 * cos_table[:, :HALF]
    cos_half[:, 0] = 1.0
    sin_half = -2.0 * sin_table[:, :HALF]
    sin_half[:, 0] = cos_table[:, HALF]
    last = np.concatenate((cos_half, sin_half), 1) / length
    twist = (np.arange(ROWS)[:, None] * ramp[None, :]) * (2.0 * np.pi / length)
    turn = np.stack((np.cos(twist), np.sin(twist))).astype(np.float32)
    return split_table(first), split_table(second), split_table(last), turn


def halves(value):
    high = value.astype(jnp.bfloat16)
    low = (value - high.astype(jnp.float32)).astype(jnp.bfloat16)
    return high, low


def dot3(left, right):
    (left_high, left_low), (right_high, right_low) = left, right
    dot = functools.partial(jnp.dot, preferred_element_type=jnp.float32)
    return dot(left_high, right_high) + (dot(left_low, right_high) + dot(left_high, right_low))


def body(
    parts,
    groups,
    each,
    block_rows,
    scale,
    kernel_in,
    sparse_in,
    target_in,
    penalty_in,
    first_in,
    second_in,
    last_in,
    turn_in,
    updated_out,
    residual_out,
    objective_out,
    terms,
    by_group,
    by_part,
    held,
    spectra,
    mid_high,
    mid_low,
    back_high,
    back_low,
    done,
    first,
    second,
    last,
    turn,
    table_sem,
    in_send,
    in_recv,
    out_send,
    out_recv,
    group_send,
    group_recv,
    part_send,
    part_recv,
):
    me = lax.axis_index("tm")
    group = lax.axis_index("ctr")
    my_rows = pl.ds(pl.multiple_of(me * block_rows, block_rows), block_rows)
    inputs = (kernel_in, sparse_in, target_in)
    outputs = (residual_out, updated_out)

    def row_of(ref, counter):
        return ref.at[lax.div(counter, 8), :, lax.rem(counter, 8)]

    def peer_rows(peer):
        return pl.ds(pl.multiple_of(peer * block_rows, block_rows), block_rows)

    def send_in(series, j, step):
        peer = lax.rem(me + step, parts)
        return pltpu.make_async_remote_copy(
            src_ref=row_of(inputs[series], peer * each + j),
            dst_ref=held.at[series, j, my_rows],
            send_sem=in_send.at[series, j, step],
            recv_sem=in_recv.at[series, j, step],
            device_id={"tm": peer},
            device_id_type=pl.DeviceIdType.MESH,
        )

    def own_in(series, j):
        return pltpu.make_async_copy(
            row_of(inputs[series], me * each + j), held.at[series, j, my_rows], in_recv.at[series, j, 0]
        )

    def send_out(which, j, step):
        peer = lax.rem(me + step, parts)
        return pltpu.make_async_remote_copy(
            src_ref=done.at[which, j, peer_rows(peer)],
            dst_ref=row_of(outputs[which], me * each + j),
            send_sem=out_send.at[which, j, step],
            recv_sem=out_recv.at[which, j, step],
            device_id={"tm": peer},
            device_id_type=pl.DeviceIdType.MESH,
        )

    def own_out(which, j):
        return pltpu.make_async_copy(
            done.at[which, j, my_rows],
            row_of(outputs[which], me * each + j),
            out_recv.at[which, j, 0],
        )

    def send_group(step):
        return pltpu.make_async_remote_copy(
            src_ref=by_group.at[group],
            dst_ref=by_group.at[group],
            send_sem=group_send.at[step],
            recv_sem=group_recv.at[step],
            device_id={"ctr": lax.rem(group + step, groups)},
            device_id_type=pl.DeviceIdType.MESH,
        )

    def send_part(step):
        return pltpu.make_async_remote_copy(
            src_ref=by_part.at[me],
            dst_ref=by_part.at[me],
            send_sem=part_send.at[step],
            recv_sem=part_recv.at[step],
            device_id={"tm": lax.rem(me + step, parts)},
            device_id_type=pl.DeviceIdType.MESH,
        )

    tables = (
        pltpu.make_async_copy(first_in, first, table_sem.at[0]),
        pltpu.make_async_copy(second_in, second, table_sem.at[1]),
        pltpu.make_async_copy(last_in, last, table_sem.at[2]),
        pltpu.make_async_copy(turn_in, turn, table_sem.at[3]),
    )
    barrier = pltpu.get_barrier_semaphore()

    @pl.loop(1, parts)
    def _(step):
        pl.semaphore_signal(
            barrier,
            inc=1,
            device_id={"tm": lax.rem(me + step, parts)},
            device_id_type=pl.DeviceIdType.MESH,
        )

    @pl.loop(1, groups)
    def _(step):
        pl.semaphore_signal(
            barrier,
            inc=1,
            device_id={"ctr": lax.rem(group + step, groups)},
            device_id_type=pl.DeviceIdType.MESH,
        )

    pl.semaphore_wait(barrier, parts + groups - 2)

    @pl.loop(0, each)
    def _(j):
        for series in range(3):

            @pl.loop(1, parts)
            def _(step):
                send_in(series, j, step).start()

            own_in(series, j).start()

    for table in tables:
        table.start()
    terms[...] = jnp.zeros_like(terms)
    for table in tables:
        table.wait()

    def send_updated(j):
        @pl.loop(1, parts)
        def _(step):
            send_out(1, j, step).start()

        own_out(1, j).start()

    def forward(series, j):
        own_in(series, j).wait()

        @pl.loop(1, parts)
        def _(step):
            send_in(series, j, step).wait_recv()

        if series == 2:

            @pl.when(j > 0)
            def _():
                send_updated(j - 1)

        for at in range(FACTOR // TILE):
            here = pl.ds(at * TILE, TILE)
            there = pl.ds(FACTOR + at * TILE, TILE)
            part = dot3((first[0], first[1]), halves(held[series, j, :, here]))
            real_part, imag_part = part[:ROWS], part[ROWS:]
            turn_cos, turn_sin = turn[0, :, here], turn[1, :, here]
            mid_high[:, here], mid_low[:, here] = halves(real_part * turn_cos + imag_part * turn_sin)
            mid_high[:, there], mid_low[:, there] = halves(
                imag_part * turn_cos - real_part * turn_sin
            )

        @pl.loop(0, 2 * FACTOR // TILE)
        def _(at):
            here = pl.ds(pl.multiple_of(at * TILE, TILE), TILE)
            spectra[series, :, here] = dot3(
                (mid_high[...], mid_low[...]), (second[0, :, here], second[1, :, here])
            )

    def spectral(at, peak):
        rows = pl.ds(pl.multiple_of(at * 16, 16), 16)
        even, odd = pl.ds(0, FACTOR), pl.ds(FACTOR, FACTOR)
        kernel_even, kernel_odd = spectra[KERNEL, rows, even], spectra[KERNEL, rows, odd]
        sparse_even, sparse_odd = spectra[SPARSE, rows, even], spectra[SPARSE, rows, odd]
        target_even, target_odd = spectra[TARGET, rows, even], spectra[TARGET, rows, odd]
        resid_even = target_even - (kernel_even * sparse_even - kernel_odd * sparse_odd)
        resid_odd = target_odd - (kernel_even * sparse_odd + kernel_odd * sparse_even)
        grad_even = kernel_even * resid_even + kernel_odd * resid_odd
        grad_odd = kernel_even * resid_odd - kernel_odd * resid_even
        back_high[0, rows, even], back_low[0, rows, even] = halves(resid_even)
        back_high[0, rows, odd], back_low[0, rows, odd] = halves(resid_odd)
        back_high[1, rows, even], back_low[1, rows, even] = halves(grad_even)
        back_high[1, rows, odd], back_low[1, rows, odd] = halves(grad_odd)
        return jnp.maximum(peak, kernel_even * kernel_even + kernel_odd * kernel_odd)

    def inverse(which, at):
        here = pl.ds(pl.multiple_of(at * TILE, TILE), TILE)
        there = pl.ds(pl.multiple_of(FACTOR + at * TILE, TILE), TILE)
        both = (back_high[which], back_low[which])
        real_part = dot3(both, (second[0, :, here], second[1, :, here]))
        imag_part = dot3(both, (second[0, :, there], second[1, :, there]))
        turn_cos, turn_sin = turn[0, :, here], turn[1, :, here]
        turned_real = real_part * turn_cos - imag_part * turn_sin
        turned_imag = (real_part * turn_sin + imag_part * turn_cos)[:HALF]
        row = lax.broadcasted_iota(jnp.int32, (HALF, TILE), 0)
        turned_imag = jnp.where(row == 0, turned_real[HALF : HALF + 1], turned_imag)
        packed = jnp.concatenate((turned_real[:HALF], turned_imag), 0)
        return here, dot3((last[0], last[1]), halves(packed))

    @pl.loop(0, each)
    def _(j):
        for series in range(3):
            forward(series, j)
        peak = lax.fori_loop(0, ROWS // 16, spectral, jnp.zeros((16, FACTOR), jnp.float32))
        peak = jnp.max(jnp.max(peak, axis=0, keepdims=True), axis=1, keepdims=True)
        step_size = 1.0 / peak
        penalty = penalty_in[me * each + j]
        limit = step_size * penalty

        @pl.loop(0, FACTOR // TILE)
        def _(at):
            here, residual = inverse(0, at)
            done[0, j, :, here] = residual
            terms[0:1, here] += jnp.sum(
                0.5 * (residual * residual) + penalty * jnp.abs(held[SPARSE, j, :, here]),
                axis=0,
                keepdims=True,
            )

        @pl.loop(1, parts)
        def _(step):
            send_out(0, j, step).start()

        own_out(0, j).start()

        @pl.when(j == each - 1)
        def _():
            total = jnp.sum(terms[...], axis=0, keepdims=True)
            total = jnp.sum(total, axis=1, keepdims=True)
            by_group[group] = jnp.broadcast_to(total, (8, 128))

            @pl.loop(1, groups)
            def _(step):
                send_group(step).start()

        @pl.loop(0, FACTOR // TILE)
        def _(at):
            here, gradient = inverse(1, at)
            moved = held[SPARSE, j, :, here] + step_size * gradient
            done[1, j, :, here] = moved - jnp.minimum(jnp.maximum(moved, -limit), limit)

    @pl.loop(1, groups)
    def _(step):
        send_group(step).wait_recv()

    total = by_group[0]
    for other in range(1, groups):
        total = total + by_group[other]
    by_part[me] = total

    @pl.loop(1, parts)
    def _(step):
        send_part(step).start()

    send_updated(each - 1)

    @pl.loop(1, parts)
    def _(step):
        send_part(step).wait_recv()

    total = by_part[0]
    for other in range(1, parts):
        total = total + by_part[other]
    objective_out[...] = total * scale

    @pl.loop(1, groups)
    def _(step):
        send_group(step).wait_send()

    @pl.loop(1, parts)
    def _(step):
        send_part(step).wait_send()

    @pl.loop(0, each)
    def _(j):
        for series in range(3):

            @pl.loop(1, parts)
            def _(step):
                send_in(series, j, step).wait_send()

        for which in range(2):
            own_out(which, j).wait()

            @pl.loop(1, parts)
            def _(step):
                send_out(which, j, step).wait()


def shards(target, sparse, kernel, penalty):
    parts = lax.axis_size("tm")
    groups = lax.axis_size("ctr")
    counters, span = sparse.shape
    each = counters // parts
    block_rows = span // FACTOR
    first, second, last, turn = make_tables()
    tiled = [x.reshape(counters // 8, 8, block_rows, FACTOR).transpose(0, 2, 1, 3) for x in (kernel, sparse, target)]
    scale = 1.0 / (span * parts * counters * groups)
    anywhere = pl.BlockSpec(memory_space=pl.ANY)
    in_vmem = pl.BlockSpec(memory_space=pltpu.VMEM)
    block = jax.ShapeDtypeStruct((counters // 8, block_rows, 8, FACTOR), jnp.float32)
    bf16, f32 = jnp.bfloat16, jnp.float32
    updated, residual, objective = pl.pallas_call(
        functools.partial(body, parts, groups, each, block_rows, scale),
        out_shape=(block, block, jax.ShapeDtypeStruct((8, 128), f32)),
        in_specs=[anywhere] * 3 + [pl.BlockSpec(memory_space=pltpu.SMEM)] + [anywhere] * 4,
        out_specs=(anywhere, anywhere, in_vmem),
        scratch_shapes=[
            pltpu.VMEM((8, FACTOR), f32),
            pltpu.VMEM((groups, 8, 128), f32),
            pltpu.VMEM((parts, 8, 128), f32),
            pltpu.VMEM((3, each, FACTOR, FACTOR), f32),
            pltpu.VMEM((3, ROWS, 2 * FACTOR), f32),
            pltpu.VMEM((ROWS, 2 * FACTOR), bf16),
            pltpu.VMEM((ROWS, 2 * FACTOR), bf16),
            pltpu.VMEM((2, ROWS, 2 * FACTOR), bf16),
            pltpu.VMEM((2, ROWS, 2 * FACTOR), bf16),
            pltpu.VMEM((2, each, FACTOR, FACTOR), f32),
            pltpu.VMEM(first.shape, bf16),
            pltpu.VMEM(second.shape, bf16),
            pltpu.VMEM(last.shape, bf16),
            pltpu.VMEM(turn.shape, f32),
            pltpu.SemaphoreType.DMA((4,)),
            pltpu.SemaphoreType.DMA((3, each, parts)),
            pltpu.SemaphoreType.DMA((3, each, parts)),
            pltpu.SemaphoreType.DMA((2, each, parts)),
            pltpu.SemaphoreType.DMA((2, each, parts)),
            pltpu.SemaphoreType.DMA((groups,)),
            pltpu.SemaphoreType.DMA((groups,)),
            pltpu.SemaphoreType.DMA((parts,)),
            pltpu.SemaphoreType.DMA((parts,)),
        ],
        compiler_params=pltpu.CompilerParams(
            collective_id=0, has_side_effects=True, vmem_limit_bytes=60 * 2**20
        ),
        cost_estimate=pl.CostEstimate(
            flops=30 * 10**9, bytes_accessed=30 * 10**6, transcendentals=0
        ),
    )(*tiled, penalty, first, second, last, turn)
    return (
        updated.transpose(0, 2, 1, 3).reshape(counters, span),
        residual.transpose(0, 2, 1, 3).reshape(counters, span),
        objective[0, 0],
    )


def solution(mesh):
    placed = (P("ctr", "tm"), P("ctr", "tm"), P("ctr", "tm"), P("ctr"))
    return jax.shard_map(
        shards,
        mesh=mesh,
        in_specs=placed,
        out_specs=(P("ctr", "tm"), P("ctr", "tm"), P()),
        check_vma=False,
    )
```
